32 devices in a mesh: groups: 2 (over y), expert: 4 (over z), et: 4 (over x, core).
Axes of the slice: x: 2, y: 2, z: 4, core: 2. Of those that a mesh axis runs over, the one named last changes fastest.
Arguments:
- tokens: bfloat16 [4096, 2048], P(('groups', 'expert', 'et')), parts along dimension 0, may hold values from -6 to 6
- grad_out: bfloat16 [4096, 2048], P(('groups', 'expert', 'et')), parts along dimension 0, may hold values from -3 to 3
- routes: int32 [4096, 1], P(('groups', 'expert', 'et')), parts along dimension 0, may hold values from 0 to 3; in each aligned block of 128 rows (0 to 127, 128 to 255, ...) at most 64 rows name the same one
- order: int32 [32, 128], P(('groups', 'expert', 'et')), parts along dimension 0, may hold values from 0 to 127, each once within a row
- w_gate: bfloat16 [4, 2048, 2048], P('expert', None, 'et'), may hold values from -0.125 to 0.125
- w_up: bfloat16 [4, 2048, 2048], P('expert', None, 'et'), may hold values from -0.125 to 0.125
- w_down: bfloat16 [4, 2048, 2048], P('expert', 'et'), may hold values from -0.125 to 0.125
Outputs:
- grad_tokens: bfloat16 [4096, 2048], P(('groups', 'expert', 'et')), parts along dimension 0
- grad_gate: bfloat16 [8, 2048, 2048], P(('groups', 'expert'), None, 'et'), parts along dimension 0
- grad_up: bfloat16 [8, 2048, 2048], P(('groups', 'expert'), None, 'et'), parts along dimension 0
- grad_down: bfloat16 [8, 2048, 2048], P(('groups', 'expert'), 'et'), parts along dimension 0
The draws below stay inside these ranges and needn't reach their ends.
There are 2 independent parts, one for each index of `groups`. The reference program is written for one: setup_inputs(seed, part) draws one part's arguments, and reference() takes and returns one part's arrays. A program takes and returns all parts, laid end to end along the dimension named above; an argument that names none is the same for every part. Nothing has to cross between parts.
Inputs may be any that keep to these rules, and one draw needn't show every extreme that they name: `routes`: in each aligned block of 128 rows (the rows of one device) no expert is named by more than 64 rows. `order`: each row holds every number of 0 to 127 once.
All inputs are finite; a program needn't handle non-finite values.
Results may differ from the reference program's by a relative error of at most 0.005.
Values may be sent and summed in bfloat16 or wider, within the bound.
No kernel may reach another device: no remote copies, remote signals or barrier semaphores. Data moves between devices by JAX's collectives and lax.ppermute only.
A program may use at most 128 MiB of HBM per device.

```python
import math
import jax
import jax.numpy as jnp
import numpy as np
from jax import lax

D = 2048
FF = 2048
TOK_DEV = 128
EXPERTS = 4
CAP = 32
MOST = 64
BLOCKS = 16
TOKENS = 2048
N_EXPERT = 4
N_ET = 4


def level_of(stream_key, shape, split, low, top_value):
    factor_of, own = 1.0, jax.random.fold_in(stream_key, 6)
    for position, shards_of in split:
        heights = jnp.exp(jax.random.uniform(jax.random.fold_in(own, position), (shards_of,), jnp.float32, low / len(split), top_value / len(split)))
        factor_of = factor_of * jnp.repeat(heights, shape[position] // shards_of).reshape([-1 if axis == position else 1 for axis in range(len(shape))])
    return factor_of


def routed_block(own_key, own, number, rows, amount, top, bound, lean):
    ranking = jax.random.permutation(own_key, amount)
    heavy_load, usual = shares(amount, rows * top, bound, lean, True), shares(amount, rows * top, bound, lean, False)
    places = jnp.arange(amount)

    def named(tallies, turn):
        used = int((tallies > 0).sum())
        fixed = max(1, used // 4)
        passed = fixed + (places - fixed + turn * (used - fixed)) % max(1, amount - fixed)
        return jnp.zeros((amount,), jnp.int32).at[ranking[jnp.where(places < fixed, places, passed)]].set(jnp.asarray(tallies, jnp.int32))

    tallies = jnp.where(number % 4 == 0, named(heavy_load, number // 4), named(usual, number - number // 4 - 1))
    mixed = jax.random.permutation(jax.random.fold_in(own, 3), amount)
    source_of, receiver = mixed[0:amount // 2 * 2:2], mixed[1:amount // 2 * 2:2]
    room = jnp.minimum(tallies[source_of] - 1, bound - tallies[receiver]) // 2
    room = jnp.where((source_of == ranking[0]) | (receiver == ranking[0]) | (tallies[receiver] == 0), 0, jnp.maximum(room, 0))
    passed = jax.random.randint(jax.random.fold_in(own, 4), (amount // 2,), 0, 1 << 20) % (room + 1)
    tallies = tallies.at[source_of].add(-passed).at[receiver].add(passed)
    labels = jnp.searchsorted(jnp.cumsum(tallies), jnp.arange(rows * top), side="right").astype(jnp.int32)
    grid = labels.reshape(top, rows).T
    grid = grid[jax.random.permutation(jax.random.fold_in(own, 1), rows)]
    turn = jax.random.randint(jax.random.fold_in(own, 2), (rows, 1), 0, top)
    return jnp.take_along_axis(grid, (jnp.arange(top)[None, :] + turn) % top, axis=1)


def shares(amount, total, bound, lean, full):
    weights = [(1 << 20) // math.isqrt(grade ** lean) + 1 for grade in range(1, amount + 1)]
    largest = bound if full else min(bound, max(-(-total // amount), total * weights[0] // sum(weights)))
    least = 1 if total - largest >= amount - 1 else 0
    holding, surplus = [largest] + [least] * (amount - 1), total - largest - least * (amount - 1)
    while surplus > 0:
        free = [i for i in range(1, amount) if holding[i] < largest] or [i for i in range(1, amount) if holding[i] < bound]
        mass, remaining = sum([weights[i] for i in free]), surplus
        for i in free:
            extra = min(bound - holding[i], max(1, remaining * weights[i] // mass), surplus)
            holding[i] = holding[i] + extra
            surplus = surplus - extra
    return np.array(holding)


def scatter_about(stream_key, extent, width, limit, pieces=(), kind=jnp.bfloat16):
    drawn = width * jax.random.normal(stream_key, extent, jnp.float32)
    if pieces:
        drawn = drawn * level_of(stream_key, extent, pieces, -0.22, 0.18)
    return jnp.clip(drawn, -limit, limit).astype(kind)


def setup_inputs(seed: int = 0, part: int = 0) -> dict:
    seeds = jax.random.split(jax.random.key(seed), 8)
    part_keys = jax.random.split(jax.random.fold_in(seeds[7], part), 8)
    tokens = scatter_about(part_keys[0], (TOKENS, D), 1.0, 6.0, ((0, 16),))
    grad_out = scatter_about(part_keys[1], (TOKENS, D), 0.2, 3.0, ((0, 16),))
    routes_keys = jax.random.split(jax.random.fold_in(part_keys[2], 1), TOKENS // TOK_DEV)
    routes_turns = jax.random.permutation(jax.random.fold_in(part_keys[2], 3), TOKENS // TOK_DEV)
    routes = jax.vmap(lambda own, number: routed_block(jax.random.fold_in(part_keys[2], 2), own, number, TOK_DEV, EXPERTS, 1, MOST, 1))(routes_keys, routes_turns).reshape((TOKENS, 1))
    order = jax.vmap(lambda own: jax.random.permutation(own, TOK_DEV))(jax.random.split(part_keys[3], BLOCKS)).reshape((BLOCKS, TOK_DEV)).astype(jnp.int32)
    w_gate = scatter_about(seeds[4], (EXPERTS, D, FF), D ** -0.5, 0.125, ((0, 4), (2, 4)))
    w_up = scatter_about(seeds[5], (EXPERTS, D, FF), D ** -0.5, 0.125, ((0, 4), (2, 4)))
    w_down = scatter_about(seeds[6], (EXPERTS, FF, D), FF ** -0.5, 0.125, ((0, 4), (1, 4)))
    return {"tokens": tokens, "grad_out": grad_out, "routes": routes, "order": order, "w_gate": w_gate, "w_up": w_up, "w_down": w_down}


def expert_backward(inputs, cotangent, gate_w, up_w, down_w):
    gate = jnp.dot(inputs, gate_w, preferred_element_type=jnp.float32)
    upper = jnp.dot(inputs, up_w, preferred_element_type=jnp.float32)
    sig = jax.nn.sigmoid(gate)
    active = gate * sig
    slope = sig * (1.0 + gate * (1.0 - sig))
    hidden = (active * upper).astype(jnp.bfloat16)
    grad_hidden = jnp.dot(cotangent, down_w.T, preferred_element_type=jnp.float32)
    grad_upper = (grad_hidden * active).astype(jnp.bfloat16)
    grad_gated = (grad_hidden * upper * slope).astype(jnp.bfloat16)
    down_grad = jnp.dot(hidden.T, cotangent, preferred_element_type=jnp.float32)
    gate_grad = jnp.dot(inputs.T, grad_gated, preferred_element_type=jnp.float32)
    up_grad = jnp.dot(inputs.T, grad_upper, preferred_element_type=jnp.float32)
    input_grad = jnp.dot(grad_gated, gate_w.T, preferred_element_type=jnp.float32) + jnp.dot(grad_upper, up_w.T, preferred_element_type=jnp.float32)
    return gate_grad, up_grad, down_grad, input_grad


def reference(tokens, grad_out, routes, order, w_gate, w_up, w_down):
    blocks = N_EXPERT * N_ET
    route = routes[:, 0].reshape(blocks, TOK_DEV)
    same = route[:, :, None] == route[:, None, :]
    earlier = order[:, None, :] < order[:, :, None]
    rank = jnp.sum((same & earlier).astype(jnp.int32), axis=2).astype(jnp.int32)
    token_id = jnp.arange(TOKENS, dtype=jnp.int32).reshape(blocks, TOK_DEV)
    block_id = jnp.broadcast_to(jnp.arange(blocks, dtype=jnp.int32)[:, None], (blocks, TOK_DEV))
    rank_slot = jnp.where(rank < CAP, rank, CAP).astype(jnp.int32)
    table = jnp.full((EXPERTS, blocks, CAP), TOKENS, jnp.int32)
    table = table.at[route, block_id, rank_slot].set(token_id, mode="drop")
    index = table.reshape(EXPERTS, blocks * CAP)
    padded_in = jnp.concatenate([tokens, jnp.zeros((1, D), tokens.dtype)], axis=0)
    padded_cot = jnp.concatenate([grad_out, jnp.zeros((1, D), grad_out.dtype)], axis=0)

    def one_expert(items):
        rows, gate_w, up_w, down_w = items
        gate_grad, up_grad, down_grad, input_grad = expert_backward(padded_in[rows], padded_cot[rows], gate_w, up_w, down_w)
        return (gate_grad.astype(jnp.bfloat16), up_grad.astype(jnp.bfloat16), down_grad.astype(jnp.bfloat16), input_grad.astype(jnp.bfloat16))

    grad_gate, grad_up, grad_down, input_rows = lax.map(one_expert, (index, w_gate, w_up, w_down))
    grad_tokens = jnp.zeros((TOKENS + 1, D), jnp.bfloat16).at[index.reshape(-1)].set(input_rows.reshape(-1, D))
    return grad_tokens[:TOKENS], grad_gate, grad_up, grad_down
```

```python
import functools

import jax
import jax.numpy as jnp
from jax import lax
from jax.experimental import pallas as pl
from jax.experimental.pallas import tpu as pltpu
from jax.sharding import PartitionSpec as P

BF16 = jnp.bfloat16
F32 = jnp.float32
GROUPS = 4
VMEM = pl.BlockSpec(memory_space=pltpu.VMEM)
NT = (((1,), (1,)), ((), ()))
TN = (((0,), (0,)), ((), ()))


def params(mib):
    return pltpu.CompilerParams(vmem_limit_bytes=mib * 1024 * 1024)


def cost(flops, moved):
    return pl.CostEstimate(flops=flops, bytes_accessed=moved, transcendentals=0)


def select_kernel(slot_cap, me, tokens, grad_out, routes, order, *outs):
    sends, back = outs[:-1], outs[-1]
    count = tokens.shape[0]
    width = tokens.shape[1]
    rows = lax.broadcasted_iota(jnp.int32, (count, count), 0)
    lanes = lax.broadcasted_iota(jnp.int32, (count, count), 1)
    eye = rows == lanes
    route_col = jnp.broadcast_to(routes[...], (count, count))
    route_row = jnp.sum(jnp.where(eye, route_col, 0), axis=0, keepdims=True)
    order_row = order[...]
    order_col = jnp.sum(jnp.where(eye, order_row, 0), axis=1, keepdims=True)
    ahead = (route_col == route_row) & (order_col < order_row)
    rank = jnp.sum(ahead.astype(jnp.int32), axis=0, keepdims=True)
    place = jnp.bitwise_xor(route_row, me[0]) * slot_cap + rank
    place = jnp.where(rank < slot_cap, place, -1)
    select = (rows == place).astype(F32).astype(BF16)
    place_col = jnp.sum(jnp.where(eye, place, 0), axis=1, keepdims=True)
    back[...] = (lanes == place_col).astype(F32).astype(BF16)
    step = count // len(sends)
    moved_in = jnp.dot(select, tokens[...], preferred_element_type=F32).astype(BF16)
    moved_cot = jnp.dot(select, grad_out[...], preferred_element_type=F32).astype(BF16)
    for g, send in enumerate(sends):
        send[:, :width] = moved_in[g * step : (g + 1) * step]
        send[:, width:] = moved_cot[g * step : (g + 1) * step]


def select_rows(tokens, grad_out, routes, order, slot_cap, me):
    count, width = tokens.shape
    step = count // GROUPS
    return pl.pallas_call(
        functools.partial(select_kernel, slot_cap),
        out_shape=[jax.ShapeDtypeStruct((step, 2 * width), BF16)] * GROUPS
        + [jax.ShapeDtypeStruct((count, count), BF16)],
        in_specs=[pl.BlockSpec(memory_space=pltpu.SMEM)] + [VMEM] * 4,
        out_specs=[VMEM] * (GROUPS + 1),
        compiler_params=params(16),
        cost_estimate=cost(4 * count * count * width, 8 * count * width),
        name="select_rows",
    )(me, tokens, grad_out, routes, order)


def chunk_kernel(n, *refs):
    blocks = refs[:n]
    gate_w, up_w, down_w = refs[n : n + 3]
    hidden_out, gated_out, upper_out, away_out, keep_out = refs[n + 3 : n + 8]
    xs, ys = refs[n + 8 :]
    rows = blocks[0].shape[0]
    width = gate_w.shape[0]
    for m, block in enumerate(blocks):
        xs[m * rows : (m + 1) * rows] = block[:, :width]
        ys[m * rows : (m + 1) * rows] = block[:, width:]
    inputs = xs[...]
    gate = jnp.dot(inputs, gate_w[...], preferred_element_type=F32)
    upper = jnp.dot(inputs, up_w[...], preferred_element_type=F32)
    sig = jax.nn.sigmoid(gate)
    active = gate * sig
    slope = sig * (1.0 + gate * (1.0 - sig))
    hidden_out[...] = (active * upper).astype(BF16)
    grad_hidden = lax.dot_general(ys[...], down_w[...], NT, preferred_element_type=F32)
    grad_upper = (grad_hidden * active).astype(BF16)
    grad_gated = (grad_hidden * upper * slope).astype(BF16)
    gated_out[...] = grad_gated
    upper_out[...] = grad_upper
    back = lax.dot_general(grad_gated, gate_w[...], NT, preferred_element_type=F32)
    back = back + lax.dot_general(grad_upper, up_w[...], NT, preferred_element_type=F32)
    for m in range(0, n, 2):
        at = m // 2 * rows
        keep_out[at : at + rows] = back[m * rows : (m + 1) * rows]
        away_out[at : at + rows] = back[(m + 1) * rows : (m + 2) * rows].astype(BF16)


def chunk_backward(blocks, gate_w, up_w, down_w):
    n = len(blocks)
    rows = blocks[0].shape[0]
    width, units = gate_w.shape
    total = n * rows
    return pl.pallas_call(
        functools.partial(chunk_kernel, n),
        out_shape=[jax.ShapeDtypeStruct((total, units), BF16)] * 3
        + [
            jax.ShapeDtypeStruct((total // 2, width), BF16),
            jax.ShapeDtypeStruct((total // 2, width), F32),
        ],
        in_specs=[VMEM] * (n + 3),
        out_specs=[VMEM] * 5,
        scratch_shapes=[pltpu.VMEM((total, width), BF16)] * 2,
        compiler_params=params(32),
        cost_estimate=cost(10 * total * width * units, 6 * width * units),
        name="chunk_backward",
    )(*blocks, gate_w, up_w, down_w)


def weights_kernel(n, *refs):
    blocks = refs[:n]
    hidden, gated, upper = (refs[n + i * GROUPS : n + (i + 1) * GROUPS] for i in range(3))
    gate_out, up_out, down_out = refs[n + 3 * GROUPS : n + 3 * GROUPS + 3]
    xs, ys, hs, gs, us = refs[n + 3 * GROUPS + 3 :]
    step = pl.program_id(0)
    rows = blocks[0].shape[0]
    width = xs.shape[1]

    @pl.when(step == 0)
    def _():
        for m, block in enumerate(blocks):
            xs[m * rows : (m + 1) * rows] = block[:, :width]
            ys[m * rows : (m + 1) * rows] = block[:, width:]
        many = hidden[0].shape[0]
        for g in range(GROUPS):
            hs[g * many : (g + 1) * many] = hidden[g][...]
            gs[g * many : (g + 1) * many] = gated[g][...]
            us[g * many : (g + 1) * many] = upper[g][...]

    part = gate_out.shape[0]
    at = pl.ds(pl.multiple_of(step * part, part), part)
    inputs = xs[:, at]
    gate_out[...] = lax.dot_general(inputs, gs[...], TN, preferred_element_type=F32).astype(BF16)
    up_out[...] = lax.dot_general(inputs, us[...], TN, preferred_element_type=F32).astype(BF16)
    down_out[...] = lax.dot_general(hs[...], ys[:, at], TN, preferred_element_type=F32).astype(BF16)


def weight_grads(blocks, hidden, gated, upper, width, units):
    n = len(blocks)
    total = n * blocks[0].shape[0]
    steps = 4
    part = width // steps

    def whole(a):
        return pl.BlockSpec(a.shape, lambda i: (0, 0))

    operands = (*blocks, *hidden, *gated, *upper)
    return pl.pallas_call(
        functools.partial(weights_kernel, n),
        grid=(steps,),
        out_shape=[
            jax.ShapeDtypeStruct((width, units), BF16),
            jax.ShapeDtypeStruct((width, units), BF16),
            jax.ShapeDtypeStruct((units, width), BF16),
        ],
        in_specs=[whole(a) for a in operands],
        out_specs=[
            pl.BlockSpec((part, units), lambda i: (i, 0)),
            pl.BlockSpec((part, units), lambda i: (i, 0)),
            pl.BlockSpec((units, part), lambda i: (0, i)),
        ],
        scratch_shapes=[pltpu.VMEM((total, width), BF16)] * 2 + [pltpu.VMEM((total, units), BF16)] * 3,
        compiler_params=params(48),
        cost_estimate=cost(6 * total * width * units, 6 * width * units),
        name="weight_grads",
    )(*operands)


def place_kernel(back, *refs):
    groups, out = refs[:-1], refs[-1]
    rows = jnp.concatenate([group[...] for group in groups], axis=0)
    out[...] = jnp.dot(back[...], rows, preferred_element_type=F32).astype(BF16)


def place_rows(back, groups):
    count, width = back.shape[0], groups[0].shape[1]
    return pl.pallas_call(
        place_kernel,
        out_shape=jax.ShapeDtypeStruct((count, width), BF16),
        in_specs=[VMEM] * (1 + len(groups)),
        out_specs=VMEM,
        compiler_params=params(16),
        cost_estimate=cost(2 * count * count * width, 4 * count * width),
        name="place_rows",
    )(back, *groups)


def on_device(tokens, grad_out, routes, order, w_gate, w_up, w_down):
    experts = lax.axis_size("expert")
    shards = lax.axis_size("et")
    local_tokens, width = tokens.shape
    slot_cap = local_tokens // experts
    per_group = experts // GROUPS
    me = lax.axis_index("expert").astype(jnp.int32).reshape(1)

    def over_expert(a, k):
        if k == 0:
            return a
        return lax.ppermute(a, "expert", [(i, i ^ k) for i in range(experts)])

    def over_et(a, m):
        return lax.ppermute(a, "et", [(i, i ^ m) for i in range(shards)])

    def exchange(a, g):
        parts = []
        for i in range(per_group):
            piece = a if per_group == 1 else a[i * slot_cap : (i + 1) * slot_cap]
            parts.append(over_expert(piece, g * per_group + i))
        return parts[0] if per_group == 1 else jnp.concatenate(parts, axis=0)

    *sends, back = select_rows(tokens, grad_out, routes, order, slot_cap, me)
    gate_w, up_w, down_w = w_gate[0], w_up[0], w_down[0]
    units = gate_w.shape[1]
    rows = local_tokens // GROUPS
    sequence = [0, 1, 3, 2]
    all_blocks, hidden, gated, upper, returned = [], [], [], [], [None] * GROUPS
    for g in sequence:
        first = exchange(sends[g], g)
        blocks = [first] + [None] * (shards - 1)
        for m in range(2, shards, 2):
            blocks[m] = over_et(first, m)
        for m in range(0, shards, 2):
            blocks[m + 1] = over_et(blocks[m], 1)
        h, gg, gu, away, keep = chunk_backward(blocks, gate_w, up_w, down_w)
        all_blocks += blocks
        hidden.append(h)
        gated.append(gg)
        upper.append(gu)
        summed = keep + over_et(away, 1).astype(F32)
        own = summed[:rows]
        for m in range(2, shards, 2):
            part = summed[m // 2 * rows : (m // 2 + 1) * rows].astype(BF16)
            own = own + over_et(part, m).astype(F32)
        returned[g] = exchange(own.astype(BF16), g)
    gate_grad, up_grad, down_grad = weight_grads(all_blocks, hidden, gated, upper, width, units)
    grad_tokens = place_rows(back, returned)
    return grad_tokens, gate_grad[None], up_grad[None], down_grad[None]


def solution(mesh):
    return jax.shard_map(
        on_device,
        mesh=mesh,
        in_specs=(
            P(("groups", "expert", "et"), None),
            P(("groups", "expert", "et"), None),
            P(("groups", "expert", "et"), None),
            P(("groups", "expert", "et"), None),
            P("expert", None, "et"),
            P("expert", None, "et"),
            P("expert", "et", None),
        ),
        out_specs=(
            P(("groups", "expert", "et"), None),
            P(("groups", "expert"), None, "et"),
            P(("groups", "expert"), None, "et"),
            P(("groups", "expert"), "et", None),
        ),
        check_vma=False,
    )
```

```python
import functools

import jax
import jax.numpy as jnp
from jax import lax
from jax.experimental import pallas as pl
from jax.experimental.pallas import tpu as pltpu
from jax.sharding import PartitionSpec as P

BF16 = jnp.bfloat16
F32 = jnp.float32
GROUPS = 4
VMEM = pl.BlockSpec(memory_space=pltpu.VMEM)
ANY = pl.BlockSpec(memory_space=pl.ANY)
HBM = pl.BlockSpec(memory_space=pltpu.HBM)
NT = (((1,), (1,)), ((), ()))
TN = (((0,), (0,)), ((), ()))
PIECES = [[(0, 0, 2), (1, 0, 2), (3, 0, 2)], [(2, 0, 2)]]
RETURNS = [[(3, 0, 2)], [(0, 0, 2), (1, 0, 2)], [(2, 0, 2)]]
PARTS = 2
CUTS = (1, 1)
GATED = True


def params(mib):
    return pltpu.CompilerParams(vmem_limit_bytes=mib * 1024 * 1024)


def cost(flops, moved):
    return pl.CostEstimate(flops=flops, bytes_accessed=moved, transcendentals=0)


def in_hbm(a):
    return pltpu.with_memory_space_constraint(a, pltpu.HBM)


def pass_kernel(*refs):
    del refs


def after(a, *others):
    return pl.pallas_call(
        pass_kernel,
        out_shape=jax.ShapeDtypeStruct(a.shape, a.dtype),
        in_specs=[ANY] * (1 + len(others)),
        out_specs=ANY,
        input_output_aliases={0: 0},
        compiler_params=params(1),
        cost_estimate=cost(0, 0),
        name="after",
    )(a, *others)


def select_kernel(slot_cap, spans, tokens, grad_out, routes, order, *refs):
    sends, back = refs[: len(spans)], refs[len(spans)]
    xs, ys, route_in, order_in, sems = refs[len(spans) + 1 :]
    small = [
        pltpu.make_async_copy(routes, route_in, sems.at[0]),
        pltpu.make_async_copy(order, order_in, sems.at[1]),
    ]
    large = [
        pltpu.make_async_copy(tokens, xs, sems.at[2]),
        pltpu.make_async_copy(grad_out, ys, sems.at[3]),
    ]
    for copy in small + large:
        copy.start()
    count, width = tokens.shape
    rows = lax.broadcasted_iota(jnp.int32, (count, count), 0)
    lanes = lax.broadcasted_iota(jnp.int32, (count, count), 1)
    eye = rows == lanes
    me = lax.axis_index("expert")
    for copy in small:
        copy.wait()
    route_row = route_in[...]
    order_row = order_in[...]
    route_col = jnp.sum(jnp.where(eye, route_row, 0), axis=1, keepdims=True)
    order_col = jnp.sum(jnp.where(eye, order_row, 0), axis=1, keepdims=True)
    ahead = (route_col == route_row) & (order_col < order_row)
    rank = jnp.sum(ahead.astype(jnp.int32), axis=0, keepdims=True)
    place = jnp.bitwise_xor(route_row, me) * slot_cap + rank
    place = jnp.where(rank < slot_cap, place, -1)
    select = (rows == place).astype(F32).astype(BF16)
    place_col = jnp.sum(jnp.where(eye, place, 0), axis=1, keepdims=True)
    back[...] = (lanes == place_col).astype(F32).astype(BF16)
    for half, copy in enumerate(large):
        copy.wait()
        moved = jnp.dot(select, (xs, ys)[half][...], preferred_element_type=F32).astype(BF16)
        for send, (low, high) in zip(sends, spans):
            send[:, half * width : (half + 1) * width] = moved[low:high]


def select_rows(tokens, grad_out, routes, order, slot_cap, spans):
    count, width = tokens.shape
    return pl.pallas_call(
        functools.partial(select_kernel, slot_cap, spans),
        out_shape=[jax.ShapeDtypeStruct((high - low, 2 * width), BF16) for low, high in spans]
        + [jax.ShapeDtypeStruct((count, count), BF16)],
        in_specs=[HBM] * 4,
        out_specs=[VMEM] * (len(spans) + 1),
        scratch_shapes=[pltpu.VMEM((count, width), BF16)] * 2
        + [pltpu.VMEM((1, count), jnp.int32)] * 2
        + [pltpu.SemaphoreType.DMA((4,))],
        compiler_params=params(16),
        cost_estimate=cost(4 * count * count * width, 8 * count * width),
        name="select_rows",
    )(*map(in_hbm, (tokens, grad_out, routes.reshape(1, count), order)))


def load_kernel(n, *refs):
    sources, targets, sems = refs[:n], refs[n + 1 : 2 * n + 1], refs[-1]
    copies = [pltpu.make_async_copy(s, t, sems.at[i]) for i, (s, t) in enumerate(zip(sources, targets))]
    for copy in copies:
        copy.start()
    for copy in copies:
        copy.wait()


def load_weights(weights, passed):
    n = len(weights)
    return pl.pallas_call(
        functools.partial(load_kernel, n),
        out_shape=[jax.ShapeDtypeStruct(a.shape, a.dtype) for a in (*weights, passed)],
        in_specs=[HBM] * n + [ANY],
        out_specs=[VMEM] * n + [ANY],
        scratch_shapes=[pltpu.SemaphoreType.DMA((n,))],
        input_output_aliases={n: n},
        compiler_params=params(2),
        cost_estimate=cost(0, 0),
        name="load_weights",
    )(*map(in_hbm, weights), passed)


def sides(blocks, width):
    left, right, parts = [], [], []
    for block in blocks:
        step = block.shape[1]
        if step == 2 * width:
            left.append(block[:, :width])
            right.append(block[:, width:])
            continue
        parts.append(block[...])
        if len(parts) * step == width:
            side = left if len(left) == len(right) else right
            side.append(parts[0] if len(parts) == 1 else jnp.concatenate(parts, axis=1))
            parts = []
    return left, right


def chunk_kernel(n, *refs):
    blocks = refs[:n]
    gate_w, up_w, down_w = refs[n : n + 3]
    hidden_out, pair_out, away_out, keep_out = refs[-4:]
    width = gate_w.shape[0]
    units = gate_w.shape[1]
    count = keep_out.shape[0]
    inputs, cotangent = (jnp.concatenate(side, axis=0) for side in sides(blocks, width))
    gate = jnp.dot(inputs, gate_w[...], preferred_element_type=F32)
    upper = jnp.dot(inputs, up_w[...], preferred_element_type=F32)
    sig = jax.nn.sigmoid(gate)
    active = gate * sig
    slope = sig * (1.0 + gate * (1.0 - sig))
    hidden_out[...] = (active * upper).astype(BF16)
    grad_hidden = lax.dot_general(cotangent, down_w[...], NT, preferred_element_type=F32)
    grad_upper = (grad_hidden * active).astype(BF16)
    grad_gated = (grad_hidden * upper * slope).astype(BF16)
    pair_out[:, :units] = grad_gated
    pair_out[:, units:] = grad_upper
    back = lax.dot_general(grad_gated, gate_w[...], NT, preferred_element_type=F32)
    back = back + lax.dot_general(grad_upper, up_w[...], NT, preferred_element_type=F32)
    keep_out[...] = back[:count]
    away_out[...] = back[count:].astype(BF16)


def chunk_backward(blocks, gate_w, up_w, down_w, *before):
    width, units = gate_w.shape
    count = sum(block.size for block in blocks) // (4 * width)
    return pl.pallas_call(
        functools.partial(chunk_kernel, len(blocks)),
        out_shape=[
            jax.ShapeDtypeStruct((2 * count, units), BF16),
            jax.ShapeDtypeStruct((2 * count, 2 * units), BF16),
            jax.ShapeDtypeStruct((count, width), BF16),
            jax.ShapeDtypeStruct((count, width), F32),
        ],
        in_specs=[VMEM] * (len(blocks) + 3) + [ANY] * len(before),
        out_specs=[VMEM] * 4,
        compiler_params=params(24),
        cost_estimate=cost(20 * count * width * units, 6 * width * units),
        name="chunk_backward",
    )(*blocks, gate_w, up_w, down_w, *before)


def gather_pieces(values, scratch):
    at = 0
    for value in values:
        scratch[at : at + value.shape[0]] = value
        at += value.shape[0]


def pair_kernel(n, *refs):
    blocks, pairs = refs[: -5 - n], refs[-5 - n : -5]
    gate_out, up_out, xs, ps = refs[-4:]
    step = pl.program_id(0)
    units = gate_out.shape[1]

    @pl.when(step == 0)
    def _():
        gather_pieces(sides(blocks, xs.shape[1])[0], xs)
        gather_pieces([pair[...] for pair in pairs], ps)

    part = gate_out.shape[0]
    inputs = xs[:, pl.ds(pl.multiple_of(step * part, part), part)]
    both = lax.dot_general(inputs, ps[...], TN, preferred_element_type=F32).astype(BF16)
    gate_out[...] = both[:, :units]
    up_out[...] = both[:, units:]


def down_kernel(n, *refs):
    blocks, hidden = refs[: -5 - n], refs[-5 - n : -5]
    down_out, mark, ys, hs = refs[-4:]
    step = pl.program_id(0)

    @pl.when(step == 0)
    def _():
        gather_pieces(sides(blocks, ys.shape[1])[1], ys)
        gather_pieces([part[...] for part in hidden], hs)
        mark[...] = jnp.zeros_like(mark)

    part = down_out.shape[1]
    cotangent = ys[:, pl.ds(pl.multiple_of(step * part, part), part)]
    down_out[...] = lax.dot_general(hs[...], cotangent, TN, preferred_element_type=F32).astype(BF16)


def whole(a):
    return pl.BlockSpec(a.shape, lambda i: (0, 0))


def pair_grads(blocks, pairs, width, units, before):
    total = sum(a.size for a in blocks) // (2 * width)
    steps = 4
    return pl.pallas_call(
        functools.partial(pair_kernel, len(pairs)),
        grid=(steps,),
        out_shape=[jax.ShapeDtypeStruct((width, units), BF16)] * 2,
        in_specs=[whole(a) for a in (*blocks, *pairs)] + [ANY],
        out_specs=[pl.BlockSpec((width // steps, units), lambda i: (i, 0))] * 2,
        scratch_shapes=[pltpu.VMEM((total, width), BF16), pltpu.VMEM((total, 2 * units), BF16)],
        compiler_params=params(32),
        cost_estimate=cost(4 * total * width * units, 4 * width * units),
        name="pair_grads",
    )(*blocks, *pairs, before)


def down_grads(blocks, hidden, width, units, before):
    total = sum(a.size for a in blocks) // (2 * width)
    steps = 4
    return pl.pallas_call(
        functools.partial(down_kernel, len(hidden)),
        grid=(steps,),
        out_shape=[jax.ShapeDtypeStruct((units, width), BF16), jax.ShapeDtypeStruct((8, 128), F32)],
        in_specs=[whole(a) for a in (*blocks, *hidden)] + [ANY],
        out_specs=[
            pl.BlockSpec((units, width // steps), lambda i: (0, i)),
            pl.BlockSpec((8, 128), lambda i: (0, 0)),
        ],
        scratch_shapes=[pltpu.VMEM((total, width), BF16), pltpu.VMEM((total, units), BF16)],
        compiler_params=params(32),
        cost_estimate=cost(2 * total * width * units, 2 * width * units),
        name="down_grads",
    )(*blocks, *hidden, before)


def place_kernel(back, *refs):
    units, out = refs[:-1], refs[-1]
    rows = jnp.concatenate([unit[...] for unit in units], axis=0)
    out[...] = jnp.dot(back[...], rows, preferred_element_type=F32).astype(BF16)


def place_rows(back, units):
    count, width = back.shape[0], units[0].shape[1]
    return pl.pallas_call(
        place_kernel,
        out_shape=jax.ShapeDtypeStruct((count, width), BF16),
        in_specs=[VMEM] * (1 + len(units)),
        out_specs=VMEM,
        compiler_params=params(16),
        cost_estimate=cost(2 * count * count * width, 4 * count * width),
        name="place_rows",
    )(back, *units)


def on_device(tokens, grad_out, routes, order, w_gate, w_up, w_down):
    experts = lax.axis_size("expert")
    shards = lax.axis_size("et")
    local_tokens, width = tokens.shape
    slot_cap = local_tokens // experts
    rows = local_tokens // GROUPS

    def over_expert(a, k):
        if k == 0:
            return a
        return lax.ppermute(a, "expert", [(i, i ^ k) for i in range(experts)])

    def over_et(a, m):
        return lax.ppermute(a, "et", [(i, i ^ m) for i in range(shards)])

    def span(unit):
        group, first, parts = unit
        low = group * rows + first * rows // PARTS
        return low, low + parts * rows // PARTS

    def exchange(a, unit):
        low, high = span(unit)
        pieces = []
        at = low
        while at < high:
            k = at // slot_cap
            end = min(high, (k + 1) * slot_cap)
            whole_unit = (at, end) == (low, high)
            pieces.append(over_expert(a if whole_unit else a[at - low : end - low], k))
            at = end
        return pieces[0] if len(pieces) == 1 else jnp.concatenate(pieces, axis=0)

    units = [unit for piece in PIECES for unit in piece]
    spans = [span(unit) for unit in units]
    *sends, back = select_rows(tokens, grad_out, routes, order, slot_cap, spans)
    sends = dict(zip(units, sends))

    arrived = {}
    for unit in units:
        arrived[unit] = exchange(sends[unit], unit)

    hidden_units = w_gate.shape[2]
    weights = None
    blocks, hidden, pairs, kept, returned = [], [], [], {}, {}
    before = []
    for step, piece in enumerate(PIECES):
        last = step == len(PIECES) - 1
        near, far = [], []
        for unit in piece:
            mine = [arrived[unit]]
            for m in range(2, shards, 2):
                mine.append(over_et(arrived[unit], m))
            if weights is None:
                *weights, mine[-1] = load_weights([w_gate[0], w_up[0], w_down[0]], mine[-1])
            if GATED and last:
                mine[-1] = after(mine[-1], *before)
            near += mine
        size = 2 * width // CUTS[step]
        far = [over_et(a[:, at : at + size], 1) for a in near for at in range(0, 2 * width, size)]
        h, pair, away, keep = chunk_backward(near + far, *weights, *before)
        before = [away]
        blocks += near + far
        hidden.append(h)
        pairs.append(pair)
        many = keep.shape[0] // len(piece)
        for i, unit in enumerate(piece):
            kept[unit] = keep[i * many : (i + 1) * many], away[i * many : (i + 1) * many]
    for group in RETURNS:
        last = group is RETURNS[-1]
        ways = shards // 2
        away = [kept[unit][1] for unit in group]
        got = over_et(away[0] if len(away) == 1 else jnp.concatenate(away, axis=0), 1).astype(F32)
        own, sent = [], [[] for _ in range(ways - 1)]
        at = 0
        for unit in group:
            keep = kept[unit][0]
            summed = keep + got[at : at + keep.shape[0]]
            at += keep.shape[0]
            many = keep.shape[0] // ways
            own.append(summed[:many])
            for w in range(1, ways):
                sent[w - 1].append(summed[w * many : (w + 1) * many].astype(BF16))
        own = jnp.concatenate(own, axis=0)
        for w, part in enumerate(sent, 1):
            part = jnp.concatenate(part, axis=0)
            own = own + over_et(part, 2 * w).astype(F32)
        own = own.astype(BF16)
        if last:
            down_grad, mark = down_grads(blocks, hidden, width, hidden_units, part)
            own = after(own, mark)
            gate_grad, up_grad = pair_grads(blocks, pairs, width, hidden_units, mark)
        at = 0
        for unit in group:
            low, high = span(unit)
            returned[unit] = exchange(own if len(group) == 1 else own[at : at + high - low], unit)
            at += high - low
    grad_tokens = place_rows(back, [returned[unit] for unit in sorted(units)])
    return grad_tokens, gate_grad[None], up_grad[None], down_grad[None]


def solution(mesh):
    return jax.shard_map(
        on_device,
        mesh=mesh,
        in_specs=(
            P(("groups", "expert", "et"), None),
            P(("groups", "expert", "et"), None),
            P(("groups", "expert", "et"), None),
            P(("groups", "expert", "et"), None),
            P("expert", None, "et"),
            P("expert", None, "et"),
            P("expert", "et", None),
        ),
        out_specs=(
            P(("groups", "expert", "et"), None),
            P(("groups", "expert"), None, "et"),
            P(("groups", "expert"), None, "et"),
            P(("groups", "expert"), "et", None),
        ),
        check_vma=False,
    )
```

```python
import functools

import jax
import jax.numpy as jnp
from jax import lax
from jax.experimental import pallas as pl
from jax.experimental.pallas import tpu as pltpu
from jax.sharding import PartitionSpec as P

BF16 = jnp.bfloat16
F32 = jnp.float32
GROUPS = 4
VMEM = pl.BlockSpec(memory_space=pltpu.VMEM)
ANY = pl.BlockSpec(memory_space=pl.ANY)
HBM = pl.BlockSpec(memory_space=pltpu.HBM)
TN = (((0,), (0,)), ((), ()))
PIECES = [[(0, 0, 2), (3, 0, 2), (1, 0, 2)], [(2, 0, 2)]]
PARTS = 2
TILES = 4
RETURNS = [[[(3, 0, 2)], [(1, 0, 2)], [(0, 0, 2)]], [[(2, 0, 2)]]]


def params(mib):
    return pltpu.CompilerParams(vmem_limit_bytes=mib * 1024 * 1024)


def cost(flops, moved):
    return pl.CostEstimate(flops=flops, bytes_accessed=moved, transcendentals=0)


def in_hbm(a):
    return pltpu.with_memory_space_constraint(a, pltpu.HBM)


def pass_kernel(*refs):
    del refs


def after(a, *others):
    return pl.pallas_call(
        pass_kernel,
        out_shape=jax.ShapeDtypeStruct(a.shape, a.dtype),
        in_specs=[ANY] * (1 + len(others)),
        out_specs=ANY,
        input_output_aliases={0: 0},
        compiler_params=params(1),
        cost_estimate=cost(0, 0),
        name="after",
    )(a, *others)


def select_kernel(slot_cap, spans, tokens, grad_out, routes, order, *refs):
    sends, back = refs[: len(spans)], refs[len(spans)]
    xs, ys, route_in, order_in, sems = refs[len(spans) + 1 :]
    small = [
        pltpu.make_async_copy(routes, route_in, sems.at[0]),
        pltpu.make_async_copy(order, order_in, sems.at[1]),
    ]
    large = [
        pltpu.make_async_copy(tokens, xs, sems.at[2]),
        pltpu.make_async_copy(grad_out, ys, sems.at[3]),
    ]
    for copy in small + large:
        copy.start()
    count, width = tokens.shape
    rows = lax.broadcasted_iota(jnp.int32, (count, count), 0)
    lanes = lax.broadcasted_iota(jnp.int32, (count, count), 1)
    eye = rows == lanes
    me = lax.axis_index("expert")
    for copy in small:
        copy.wait()
    route_row = route_in[...]
    order_row = order_in[...]
    route_col = jnp.sum(jnp.where(eye, route_row, 0), axis=1, keepdims=True)
    order_col = jnp.sum(jnp.where(eye, order_row, 0), axis=1, keepdims=True)
    ahead = (route_col == route_row) & (order_col < order_row)
    rank = jnp.sum(ahead.astype(jnp.int32), axis=0, keepdims=True)
    place = jnp.bitwise_xor(route_row, me) * slot_cap + rank
    place = jnp.where(rank < slot_cap, place, -1)
    select = (rows == place).astype(F32).astype(BF16)
    place_col = jnp.sum(jnp.where(eye, place, 0), axis=1, keepdims=True)
    back[...] = (lanes == place_col).astype(F32).astype(BF16)
    for half, copy in enumerate(large):
        copy.wait()
        moved = jnp.dot(select, (xs, ys)[half][...], preferred_element_type=F32).astype(BF16)
        for send, (low, high) in zip(sends, spans):
            send[:, half * width : (half + 1) * width] = moved[low:high]


def select_rows(tokens, grad_out, routes, order, slot_cap, spans):
    count, width = tokens.shape
    return pl.pallas_call(
        functools.partial(select_kernel, slot_cap, spans),
        out_shape=[jax.ShapeDtypeStruct((high - low, 2 * width), BF16) for low, high in spans]
        + [jax.ShapeDtypeStruct((count, count), BF16)],
        in_specs=[HBM] * 4,
        out_specs=[VMEM] * (len(spans) + 1),
        scratch_shapes=[pltpu.VMEM((count, width), BF16)] * 2
        + [pltpu.VMEM((1, count), jnp.int32)] * 2
        + [pltpu.SemaphoreType.DMA((4,))],
        compiler_params=params(16),
        cost_estimate=cost(4 * count * count * width, 8 * count * width),
        name="select_rows",
    )(*map(in_hbm, (tokens, grad_out, routes.reshape(1, count), order)))


def load_kernel(gate_w, up_w, down_w, passed, pair_w, pair_t, down_t, passed_out, down_in, sems):
    del passed, passed_out
    width, units = gate_w.shape
    copies = [
        pltpu.make_async_copy(down_w, down_in, sems.at[0]),
        pltpu.make_async_copy(gate_w, pair_w.at[:, pl.ds(0, units)], sems.at[1]),
        pltpu.make_async_copy(up_w, pair_w.at[:, pl.ds(units, units)], sems.at[2]),
    ]
    for copy in copies:
        copy.start()
    tiles = width // units
    copies[0].wait()
    for t in range(tiles):
        part = slice(t * units, (t + 1) * units)
        down_t[part] = down_in[:, part].T
    for half in range(2):
        copies[1 + half].wait()
        side = slice(half * units, (half + 1) * units)
        for t in range(tiles):
            part = slice(t * units, (t + 1) * units)
            pair_t[side, part] = pair_w[part, side].T


def load_weights(gate_w, up_w, down_w, passed):
    width, units = gate_w.shape
    return pl.pallas_call(
        load_kernel,
        out_shape=[
            jax.ShapeDtypeStruct((width, 2 * units), BF16),
            jax.ShapeDtypeStruct((2 * units, width), BF16),
            jax.ShapeDtypeStruct((width, units), BF16),
            jax.ShapeDtypeStruct(passed.shape, passed.dtype),
        ],
        in_specs=[HBM] * 3 + [ANY],
        out_specs=[VMEM] * 3 + [ANY],
        scratch_shapes=[pltpu.VMEM((units, width), BF16), pltpu.SemaphoreType.DMA((3,))],
        input_output_aliases={3: 3},
        compiler_params=params(12),
        cost_estimate=cost(0, 0),
        name="load_weights",
    )(*map(in_hbm, (gate_w, up_w, down_w)), passed)


def chunk_kernel(n, first, *refs):
    blocks = refs[:n]
    pair_w, pair_t, down_t = refs[n : n + 3]
    xs, ys, hs, ps, away_out, keep_out = refs[-6:]
    width = pair_w.shape[0]
    units = down_t.shape[1]
    count = keep_out.shape[0]
    at = first
    for block in blocks:
        rows = block.shape[0]
        xs[at : at + rows] = block[:, :width]
        ys[at : at + rows] = block[:, width:]
        at += rows
    mine = slice(first, at)
    both = jnp.dot(xs[mine], pair_w[...], preferred_element_type=F32)
    gate, upper = both[:, :units], both[:, units:]
    sig = jax.nn.sigmoid(gate)
    active = gate * sig
    slope = sig * (1.0 + gate * (1.0 - sig))
    hs[mine] = (active * upper).astype(BF16)
    grad_hidden = jnp.dot(ys[mine], down_t[...], preferred_element_type=F32)
    ps[mine, :units] = (grad_hidden * upper * slope).astype(BF16)
    ps[mine, units:] = (grad_hidden * active).astype(BF16)
    back = jnp.dot(ps[mine], pair_t[...], preferred_element_type=F32)
    keep_out[...] = back[:count]
    away_out[...] = back[count:].astype(BF16)


def chunk_backward(blocks, weights, first, total, earlier, gates):
    n = len(blocks)
    width, units = weights[2].shape
    count = sum(block.shape[0] for block in blocks) // 2
    aliases = {n + 3 + i: i for i in range(len(earlier))}
    return pl.pallas_call(
        functools.partial(chunk_kernel, n, first),
        out_shape=[
            jax.ShapeDtypeStruct((total, width), BF16),
            jax.ShapeDtypeStruct((total, width), BF16),
            jax.ShapeDtypeStruct((total, units), BF16),
            jax.ShapeDtypeStruct((total, 2 * units), BF16),
            jax.ShapeDtypeStruct((count, width), BF16),
            jax.ShapeDtypeStruct((count, width), F32),
        ],
        in_specs=[VMEM] * (n + 3 + len(earlier)) + [ANY] * len(gates),
        out_specs=[VMEM] * 6,
        input_output_aliases=aliases,
        compiler_params=params(16),
        cost_estimate=cost(20 * count * width * units, 6 * width * units),
        name="chunk_backward",
    )(*blocks, *weights, *earlier, *gates)


def pair_kernel(xs, ps, before, gate_out, up_out, results, sems):
    del before
    units = gate_out.shape[1]
    part = xs.shape[1] // TILES
    copies = []
    for t in range(TILES):
        rows = slice(t * part, (t + 1) * part)
        both = lax.dot_general(xs[:, rows], ps[...], TN, preferred_element_type=F32)
        results[rows] = both.astype(BF16)
        for i, out in enumerate((gate_out, up_out)):
            source = results.at[pl.ds(t * part, part), pl.ds(i * units, units)]
            copies.append(pltpu.make_async_copy(source, out.at[pl.ds(t * part, part)], sems.at[t, i]))
            copies[-1].start()
    for copy in copies:
        copy.wait()


def down_kernel(ys, hs, before, down_out, mark, results, sems):
    del before
    mark[...] = jnp.zeros_like(mark)
    part = ys.shape[1] // TILES
    copies = []
    for t in range(TILES):
        columns = slice(t * part, (t + 1) * part)
        tile = lax.dot_general(hs[...], ys[:, columns], TN, preferred_element_type=F32)
        results[:, columns] = tile.astype(BF16)
        place = pl.ds(t * part, part)
        copies.append(pltpu.make_async_copy(results.at[:, place], down_out.at[:, place], sems.at[t]))
        copies[-1].start()
    for copy in copies:
        copy.wait()


def pair_grads(xs, ps, before):
    total, width = xs.shape
    units = ps.shape[1] // 2
    return pl.pallas_call(
        pair_kernel,
        out_shape=[jax.ShapeDtypeStruct((width, units), BF16)] * 2,
        in_specs=[VMEM, VMEM, ANY],
        out_specs=[HBM] * 2,
        scratch_shapes=[pltpu.VMEM((width, 2 * units), BF16), pltpu.SemaphoreType.DMA((TILES, 2))],
        compiler_params=params(16),
        cost_estimate=cost(4 * total * width * units, 4 * width * units),
        name="pair_grads",
    )(xs, ps, before)


def down_grads(ys, hs, before):
    total, width = ys.shape
    units = hs.shape[1]
    return pl.pallas_call(
        down_kernel,
        out_shape=[jax.ShapeDtypeStruct((units, width), BF16), jax.ShapeDtypeStruct((8, 128), F32)],
        in_specs=[VMEM, VMEM, ANY],
        out_specs=[HBM, VMEM],
        scratch_shapes=[pltpu.VMEM((units, width), BF16), pltpu.SemaphoreType.DMA((TILES,))],
        compiler_params=params(12),
        cost_estimate=cost(2 * total * width * units, 2 * width * units),
        name="down_grads",
    )(ys, hs, before)


def place_kernel(back, *refs):
    units, out = refs[:-1], refs[-1]
    rows = jnp.concatenate([unit[...] for unit in units], axis=0)
    out[...] = jnp.dot(back[...], rows, preferred_element_type=F32).astype(BF16)


def place_rows(back, units):
    count, width = back.shape[0], units[0].shape[1]
    return pl.pallas_call(
        place_kernel,
        out_shape=jax.ShapeDtypeStruct((count, width), BF16),
        in_specs=[VMEM] * (1 + len(units)),
        out_specs=VMEM,
        compiler_params=params(16),
        cost_estimate=cost(2 * count * count * width, 4 * count * width),
        name="place_rows",
    )(back, *units)


def on_device(tokens, grad_out, routes, order, w_gate, w_up, w_down):
    experts = lax.axis_size("expert")
    shards = lax.axis_size("et")
    local_tokens, width = tokens.shape
    slot_cap = local_tokens // experts
    rows = local_tokens // GROUPS

    def over_expert(a, k):
        if k == 0:
            return a
        return lax.ppermute(a, "expert", [(i, i ^ k) for i in range(experts)])

    def over_et(a, m):
        return lax.ppermute(a, "et", [(i, i ^ m) for i in range(shards)])

    def span(unit):
        group, first, parts = unit
        low = group * rows + first * rows // PARTS
        return low, low + parts * rows // PARTS

    def exchange(a, unit):
        low, high = span(unit)
        pieces = []
        at = low
        while at < high:
            k = at // slot_cap
            end = min(high, (k + 1) * slot_cap)
            whole_unit = (at, end) == (low, high)
            pieces.append(over_expert(a if whole_unit else a[at - low : end - low], k))
            at = end
        return pieces[0] if len(pieces) == 1 else jnp.concatenate(pieces, axis=0)

    units = [unit for piece in PIECES for unit in piece]
    spans = [span(unit) for unit in units]
    *sends, back = select_rows(tokens, grad_out, routes, order, slot_cap, spans)
    sends = dict(zip(units, sends))

    arrived = {}
    for unit in units:
        arrived[unit] = exchange(sends[unit], unit)

    weights = None
    ways = shards // 2
    kept, returned = {}, {}
    before, gates, returns = [], [], []
    everything, first = [], 0
    for step, piece in enumerate(PIECES):
        last = step == len(PIECES) - 1
        near = []
        for unit in piece:
            mine = [arrived[unit]]
            for m in range(2, shards, 2):
                mine.append(over_et(arrived[unit], m))
            if weights is None:
                *weights, mine[-1] = load_weights(w_gate[0], w_up[0], w_down[0], mine[-1])
            if last:
                mine[-1] = after(mine[-1], *before)
            near += mine
        far = [over_et(a, 1) for a in near]
        *everything, away, keep = chunk_backward(
            near + far, weights, first, shards * local_tokens, everything, before + gates
        )
        first += 2 * keep.shape[0]
        before = [away]
        many = keep.shape[0] // len(piece)
        for i, unit in enumerate(piece):
            kept[unit] = keep[i * many : (i + 1) * many], away[i * many : (i + 1) * many]
        for group in RETURNS[step]:
            own, sent = [], [[] for _ in range(ways - 1)]
            for unit in group:
                keep, away = kept[unit]
                summed = keep + over_et(away, 1).astype(F32)
                many = keep.shape[0] // ways
                own.append(summed[:many])
                for w in range(1, ways):
                    sent[w - 1].append(summed[w * many : (w + 1) * many].astype(BF16))
            own = jnp.concatenate(own, axis=0)
            sent = [jnp.concatenate(part, axis=0) for part in sent]
            if not gates:
                gates.append(sent[-1])
            returns.append((group, own, sent))
    xs, ys, hs, ps = everything
    down_grad, mark = down_grads(ys, hs, returns[-1][2][-1])
    part = returns[-1][2][-1]
    done = {}
    group, own, sent = returns[0]
    for w, piece in enumerate(sent, 1):
        own = own + over_et(piece, 2 * w).astype(F32)
    own = own.astype(BF16)
    done[0] = own
    at = 0
    for unit in group:
        low, high = span(unit)
        returned[unit] = exchange(own if len(group) == 1 else own[at : at + high - low], unit)
        at += high - low
    group, own, sent = returns[3]
    for w, piece in enumerate(sent, 1):
        own = own + over_et(piece, 2 * w).astype(F32)
    own = own.astype(BF16)
    own = after(own, mark)
    done[3] = own
    at = 0
    for unit in group:
        low, high = span(unit)
        returned[unit] = exchange(own if len(group) == 1 else own[at : at + high - low], unit)
        at += high - low
    group, own, sent = returns[1]
    for w, piece in enumerate(sent, 1):
        own = own + over_et(piece, 2 * w).astype(F32)
    own = own.astype(BF16)
    own = after(own, done[3])
    done[1] = own
    at = 0
    for unit in group:
        low, high = span(unit)
        returned[unit] = exchange(own if len(group) == 1 else own[at : at + high - low], unit)
        at += high - low
    group, own, sent = returns[2]
    sent = [after(piece, done[3]) for piece in sent]
    for w, piece in enumerate(sent, 1):
        own = own + over_et(piece, 2 * w).astype(F32)
    own = own.astype(BF16)
    done[2] = own
    at = 0
    for unit in group:
        low, high = span(unit)
        returned[unit] = exchange(own if len(group) == 1 else own[at : at + high - low], unit)
        at += high - low
    gate_grad, up_grad = pair_grads(xs, ps, done[3])
    grad_tokens = place_rows(back, [returned[unit] for unit in sorted(units)])
    return grad_tokens, gate_grad[None], up_grad[None], down_grad[None]


def solution(mesh):
    return jax.shard_map(
        on_device,
        mesh=mesh,
        in_specs=(
            P(("groups", "expert", "et"), None),
            P(("groups", "expert", "et"), None),
            P(("groups", "expert", "et"), None),
            P(("groups", "expert", "et"), None),
            P("expert", None, "et"),
            P("expert", None, "et"),
            P("expert", "et", None),
        ),
        out_specs=(
            P(("groups", "expert", "et"), None),
            P(("groups", "expert"), None, "et"),
            P(("groups", "expert"), None, "et"),
            P(("groups", "expert"), "et", None),
        ),
        check_vma=False,
    )
```

```python
import functools

import jax
import jax.numpy as jnp
from jax import lax
from jax.experimental import pallas as pl
from jax.experimental.pallas import tpu as pltpu
from jax.sharding import PartitionSpec as P

BF16 = jnp.bfloat16
F32 = jnp.float32
GROUPS = 4
VMEM = pl.BlockSpec(memory_space=pltpu.VMEM)
ANY = pl.BlockSpec(memory_space=pl.ANY)
HBM = pl.BlockSpec(memory_space=pltpu.HBM)
TN = (((0,), (0,)), ((), ()))
PIECES = [[(0, 0, 2), (3, 0, 2), (1, 0, 2)], [(2, 0, 2)]]
PARTS = 2
TILES = 4
RETURNS = [[[(3, 0, 2)], [(1, 0, 2)], [(0, 0, 2)]], [[(2, 0, 2)]]]


def params(mib):
    return pltpu.CompilerParams(vmem_limit_bytes=mib * 1024 * 1024)


def cost(flops, moved):
    return pl.CostEstimate(flops=flops, bytes_accessed=moved, transcendentals=0)


def in_hbm(a):
    return pltpu.with_memory_space_constraint(a, pltpu.HBM)


def pass_kernel(*refs):
    del refs


def after(a, *others):
    return pl.pallas_call(
        pass_kernel,
        out_shape=jax.ShapeDtypeStruct(a.shape, a.dtype),
        in_specs=[ANY] * (1 + len(others)),
        out_specs=ANY,
        input_output_aliases={0: 0},
        compiler_params=params(1),
        cost_estimate=cost(0, 0),
        name="after",
    )(a, *others)


def select_kernel(slot_cap, spans, tokens, grad_out, routes, order, *refs):
    sends, back = refs[: len(spans)], refs[len(spans)]
    xs, ys, route_in, order_in, sems = refs[len(spans) + 1 :]
    small = [
        pltpu.make_async_copy(routes, route_in, sems.at[0]),
        pltpu.make_async_copy(order, order_in, sems.at[1]),
    ]
    large = [
        pltpu.make_async_copy(tokens, xs, sems.at[2]),
        pltpu.make_async_copy(grad_out, ys, sems.at[3]),
    ]
    for copy in small + large:
        copy.start()
    count, width = tokens.shape
    rows = lax.broadcasted_iota(jnp.int32, (count, count), 0)
    lanes = lax.broadcasted_iota(jnp.int32, (count, count), 1)
    eye = rows == lanes
    me = lax.axis_index("expert")
    for copy in small:
        copy.wait()
    route_row = route_in[...]
    order_row = order_in[...]
    route_col = jnp.sum(jnp.where(eye, route_row, 0), axis=1, keepdims=True)
    order_col = jnp.sum(jnp.where(eye, order_row, 0), axis=1, keepdims=True)
    ahead = (route_col == route_row) & (order_col < order_row)
    rank = jnp.sum(ahead.astype(jnp.int32), axis=0, keepdims=True)
    place = jnp.bitwise_xor(route_row, me) * slot_cap + rank
    place = jnp.where(rank < slot_cap, place, -1)
    select = (rows == place).astype(F32).astype(BF16)
    place_col = jnp.sum(jnp.where(eye, place, 0), axis=1, keepdims=True)
    back[...] = (lanes == place_col).astype(F32).astype(BF16)
    for half, copy in enumerate(large):
        copy.wait()
        moved = jnp.dot(select, (xs, ys)[half][...], preferred_element_type=F32).astype(BF16)
        for send, (low, high) in zip(sends, spans):
            send[:, half * width : (half + 1) * width] = moved[low:high]


def select_rows(tokens, grad_out, routes, order, slot_cap, spans):
    count, width = tokens.shape
    return pl.pallas_call(
        functools.partial(select_kernel, slot_cap, spans),
        out_shape=[jax.ShapeDtypeStruct((high - low, 2 * width), BF16) for low, high in spans]
        + [jax.ShapeDtypeStruct((count, count), BF16)],
        in_specs=[HBM] * 4,
        out_specs=[VMEM] * (len(spans) + 1),
        scratch_shapes=[pltpu.VMEM((count, width), BF16)] * 2
        + [pltpu.VMEM((1, count), jnp.int32)] * 2
        + [pltpu.SemaphoreType.DMA((4,))],
        compiler_params=params(16),
        cost_estimate=cost(4 * count * count * width, 8 * count * width),
        name="select_rows",
    )(*map(in_hbm, (tokens, grad_out, routes.reshape(1, count), order)))


def load_kernel(gate_w, up_w, down_w, passed, pair_w, pair_t, down_t, passed_out, down_in, sems):
    del passed, passed_out
    width, units = gate_w.shape
    copies = [
        pltpu.make_async_copy(down_w, down_in, sems.at[0]),
        pltpu.make_async_copy(gate_w, pair_w.at[:, pl.ds(0, units)], sems.at[1]),
        pltpu.make_async_copy(up_w, pair_w.at[:, pl.ds(units, units)], sems.at[2]),
    ]
    for copy in copies:
        copy.start()
    tiles = width // units
    copies[0].wait()
    for t in range(tiles):
        part = slice(t * units, (t + 1) * units)
        down_t[part] = down_in[:, part].T
    for half in range(2):
        copies[1 + half].wait()
        side = slice(half * units, (half + 1) * units)
        for t in range(tiles):
            part = slice(t * units, (t + 1) * units)
            pair_t[side, part] = pair_w[part, side].T


def load_weights(gate_w, up_w, down_w, passed):
    width, units = gate_w.shape
    return pl.pallas_call(
        load_kernel,
        out_shape=[
            jax.ShapeDtypeStruct((width, 2 * units), BF16),
            jax.ShapeDtypeStruct((2 * units, width), BF16),
            jax.ShapeDtypeStruct((width, units), BF16),
            jax.ShapeDtypeStruct(passed.shape, passed.dtype),
        ],
        in_specs=[HBM] * 3 + [ANY],
        out_specs=[VMEM] * 3 + [ANY],
        scratch_shapes=[pltpu.VMEM((units, width), BF16), pltpu.SemaphoreType.DMA((3,))],
        input_output_aliases={3: 3},
        compiler_params=params(12),
        cost_estimate=cost(0, 0),
        name="load_weights",
    )(*map(in_hbm, (gate_w, up_w, down_w)), passed)


def chunk_kernel(n, first, *refs):
    blocks = refs[:n]
    pair_w, pair_t, down_t = refs[n : n + 3]
    xs, ys, hs, ps, away_out, keep_out = refs[-6:]
    width = pair_w.shape[0]
    units = down_t.shape[1]
    count = keep_out.shape[0]
    at = first
    for block in blocks:
        rows = block.shape[0]
        xs[at : at + rows] = block[:, :width]
        ys[at : at + rows] = block[:, width:]
        at += rows
    mine = slice(first, at)
    both = jnp.dot(xs[mine], pair_w[...], preferred_element_type=F32)
    gate, upper = both[:, :units], both[:, units:]
    sig = jax.nn.sigmoid(gate)
    active = gate * sig
    slope = sig * (1.0 + gate * (1.0 - sig))
    hs[mine] = (active * upper).astype(BF16)
    grad_hidden = jnp.dot(ys[mine], down_t[...], preferred_element_type=F32)
    ps[mine, :units] = (grad_hidden * upper * slope).astype(BF16)
    ps[mine, units:] = (grad_hidden * active).astype(BF16)
    back = jnp.dot(ps[mine], pair_t[...], preferred_element_type=F32)
    keep_out[...] = back[:count]
    away_out[...] = back[count:].astype(BF16)


def chunk_backward(blocks, weights, first, total, earlier, gates):
    n = len(blocks)
    width, units = weights[2].shape
    count = sum(block.shape[0] for block in blocks) // 2
    aliases = {n + 3 + i: i for i in range(len(earlier))}
    return pl.pallas_call(
        functools.partial(chunk_kernel, n, first),
        out_shape=[
            jax.ShapeDtypeStruct((total, width), BF16),
            jax.ShapeDtypeStruct((total, width), BF16),
            jax.ShapeDtypeStruct((total, units), BF16),
            jax.ShapeDtypeStruct((total, 2 * units), BF16),
            jax.ShapeDtypeStruct((count, width), BF16),
            jax.ShapeDtypeStruct((count, width), F32),
        ],
        in_specs=[VMEM] * (n + 3 + len(earlier)) + [ANY] * len(gates),
        out_specs=[VMEM] * 6,
        input_output_aliases=aliases,
        compiler_params=params(16),
        cost_estimate=cost(20 * count * width * units, 6 * width * units),
        name="chunk_backward",
    )(*blocks, *weights, *earlier, *gates)


def pair_kernel(xs, ps, before, gate_out, up_out, results, sems):
    del before
    units = gate_out.shape[1]
    part = xs.shape[1] // TILES
    copies = []
    for t in range(TILES):
        rows = slice(t * part, (t + 1) * part)
        both = lax.dot_general(xs[:, rows], ps[...], TN, preferred_element_type=F32)
        results[rows] = both.astype(BF16)
        for i, out in enumerate((gate_out, up_out)):
            source = results.at[pl.ds(t * part, part), pl.ds(i * units, units)]
            copies.append(pltpu.make_async_copy(source, out.at[pl.ds(t * part, part)], sems.at[t, i]))
            copies[-1].start()
    for copy in copies:
        copy.wait()


def down_kernel(ys, hs, before, down_out, mark, results, sems):
    del before
    mark[...] = jnp.zeros_like(mark)
    part = ys.shape[1] // TILES
    copies = []
    for t in range(TILES):
        columns = slice(t * part, (t + 1) * part)
        tile = lax.dot_general(hs[...], ys[:, columns], TN, preferred_element_type=F32)
        results[:, columns] = tile.astype(BF16)
        place = pl.ds(t * part, part)
        copies.append(pltpu.make_async_copy(results.at[:, place], down_out.at[:, place], sems.at[t]))
        copies[-1].start()
    for copy in copies:
        copy.wait()


def pair_grads(xs, ps, before):
    total, width = xs.shape
    units = ps.shape[1] // 2
    return pl.pallas_call(
        pair_kernel,
        out_shape=[jax.ShapeDtypeStruct((width, units), BF16)] * 2,
        in_specs=[VMEM, VMEM, ANY],
        out_specs=[HBM] * 2,
        scratch_shapes=[pltpu.VMEM((width, 2 * units), BF16), pltpu.SemaphoreType.DMA((TILES, 2))],
        compiler_params=params(16),
        cost_estimate=cost(4 * total * width * units, 4 * width * units),
        name="pair_grads",
    )(xs, ps, before)


def down_grads(ys, hs, before):
    total, width = ys.shape
    units = hs.shape[1]
    return pl.pallas_call(
        down_kernel,
        out_shape=[jax.ShapeDtypeStruct((units, width), BF16), jax.ShapeDtypeStruct((8, 128), F32)],
        in_specs=[VMEM, VMEM, ANY],
        out_specs=[HBM, VMEM],
        scratch_shapes=[pltpu.VMEM((units, width), BF16), pltpu.SemaphoreType.DMA((TILES,))],
        compiler_params=params(12),
        cost_estimate=cost(2 * total * width * units, 2 * width * units),
        name="down_grads",
    )(ys, hs, before)


def place_kernel(back, *refs):
    units, (out, results, sems) = refs[:-3], refs[-3:]
    part = out.shape[1] // TILES
    copies = []
    for t in range(TILES):
        columns = pl.ds(t * part, part)
        rows = jnp.concatenate([unit[:, columns] for unit in units], axis=0)
        results[:, columns] = jnp.dot(back[...], rows, preferred_element_type=F32).astype(BF16)
        copies.append(pltpu.make_async_copy(results.at[:, columns], out.at[:, columns], sems.at[t]))
        copies[-1].start()
    for copy in copies:
        copy.wait()


def place_rows(back, units):
    count, width = back.shape[0], units[0].shape[1]
    return pl.pallas_call(
        place_kernel,
        out_shape=jax.ShapeDtypeStruct((count, width), BF16),
        in_specs=[VMEM] * (1 + len(units)),
        out_specs=HBM,
        scratch_shapes=[pltpu.VMEM((count, width), BF16), pltpu.SemaphoreType.DMA((TILES,))],
        compiler_params=params(16),
        cost_estimate=cost(2 * count * count * width, 4 * count * width),
        name="place_rows",
    )(back, *units)


def on_device(tokens, grad_out, routes, order, w_gate, w_up, w_down):
    experts = lax.axis_size("expert")
    shards = lax.axis_size("et")
    local_tokens, width = tokens.shape
    slot_cap = local_tokens // experts
    rows = local_tokens // GROUPS

    def over_expert(a, k):
        if k == 0:
            return a
        return lax.ppermute(a, "expert", [(i, i ^ k) for i in range(experts)])

    def over_et(a, m):
        return lax.ppermute(a, "et", [(i, i ^ m) for i in range(shards)])

    def span(unit):
        group, first, parts = unit
        low = group * rows + first * rows // PARTS
        return low, low + parts * rows // PARTS

    def exchange(a, unit):
        low, high = span(unit)
        pieces = []
        at = low
        while at < high:
            k = at // slot_cap
            end = min(high, (k + 1) * slot_cap)
            whole_unit = (at, end) == (low, high)
            pieces.append(over_expert(a if whole_unit else a[at - low : end - low], k))
            at = end
        return pieces[0] if len(pieces) == 1 else jnp.concatenate(pieces, axis=0)

    units = [unit for piece in PIECES for unit in piece]
    spans = [span(unit) for unit in units]
    *sends, back = select_rows(tokens, grad_out, routes, order, slot_cap, spans)
    sends = dict(zip(units, sends))

    arrived = {}
    for unit in units:
        arrived[unit] = exchange(sends[unit], unit)

    weights = None
    ways = shards // 2
    kept, returned = {}, {}
    before, gates, returns = [], [], []
    everything, first = [], 0
    for step, piece in enumerate(PIECES):
        last = step == len(PIECES) - 1
        near = []
        for unit in piece:
            mine = [arrived[unit]]
            for m in range(2, shards, 2):
                mine.append(over_et(arrived[unit], m))
            if weights is None:
                *weights, mine[-1] = load_weights(w_gate[0], w_up[0], w_down[0], mine[-1])
            if last:
                mine[-1] = after(mine[-1], *before)
            near += mine
        far = [over_et(a, 1) for a in near]
        *everything, away, keep = chunk_backward(
            near + far, weights, first, shards * local_tokens, everything, before + gates
        )
        first += 2 * keep.shape[0]
        before = [away]
        many = keep.shape[0] // len(piece)
        for i, unit in enumerate(piece):
            kept[unit] = keep[i * many : (i + 1) * many], away[i * many : (i + 1) * many]
        for group in RETURNS[step]:
            own, sent = [], [[] for _ in range(ways - 1)]
            for unit in group:
                keep, away = kept[unit]
                summed = keep + over_et(away, 1).astype(F32)
                many = keep.shape[0] // ways
                own.append(summed[:many])
                for w in range(1, ways):
                    sent[w - 1].append(summed[w * many : (w + 1) * many].astype(BF16))
            own = jnp.concatenate(own, axis=0)
            sent = [jnp.concatenate(part, axis=0) for part in sent]
            if not gates:
                gates.append(sent[-1])
            returns.append((group, own, sent))
    xs, ys, hs, ps = everything
    down_grad, mark = down_grads(ys, hs, returns[-1][2][-1])
    done = {}
    for k in (0, 3, 1, 2):
        _, own, sent = returns[k]
        if k == 2:
            sent = [after(piece, mark) for piece in sent]
        for w, piece in enumerate(sent, 1):
            own = own + over_et(piece, 2 * w).astype(F32)
        done[k] = own.astype(BF16)
    for k, gate in ((0, None), (3, mark), (1, 3), (2, None)):
        if gate is not None:
            done[k] = after(done[k], done[gate] if k == 1 else gate)
        (unit,) = returns[k][0]
        returned[unit] = exchange(done[k], unit)
    gate_grad, up_grad = pair_grads(xs, ps, done[3])
    grad_tokens = place_rows(back, [returned[unit] for unit in sorted(units)])
    return grad_tokens, gate_grad[None], up_grad[None], down_grad[None]


def solution(mesh):
    return jax.shard_map(
        on_device,
        mesh=mesh,
        in_specs=(
            P(("groups", "expert", "et"), None),
            P(("groups", "expert", "et"), None),
            P(("groups", "expert", "et"), None),
            P(("groups", "expert", "et"), None),
            P("expert", None, "et"),
            P("expert", None, "et"),
            P("expert", "et", None),
        ),
        out_specs=(
            P(("groups", "expert", "et"), None),
            P(("groups", "expert"), None, "et"),
            P(("groups", "expert"), None, "et"),
            P(("groups", "expert"), "et", None),
        ),
        check_vma=False,
    )
```

```python
import functools

import jax
import jax.numpy as jnp
from jax import lax
from jax.experimental import pallas as pl
from jax.experimental.pallas import tpu as pltpu
from jax.sharding import PartitionSpec as P

BF16 = jnp.bfloat16
F32 = jnp.float32
GROUPS = 4
VMEM = pl.BlockSpec(memory_space=pltpu.VMEM)
ANY = pl.BlockSpec(memory_space=pl.ANY)
HBM = pl.BlockSpec(memory_space=pltpu.HBM)
TN = (((0,), (0,)), ((), ()))
PIECES = [[(0, 0, 2), (3, 0, 2), (1, 0, 2)], [(2, 0, 2)]]
PARTS = 2
TILES = 4
PAIR_TILES = 8
RETURNS = [[[(3, 0, 2)], [(1, 0, 2)], [(0, 0, 2)]], [[(2, 0, 2)]]]


def params(mib):
    return pltpu.CompilerParams(vmem_limit_bytes=mib * 1024 * 1024)


def cost(flops, moved):
    return pl.CostEstimate(flops=flops, bytes_accessed=moved, transcendentals=0)


def in_hbm(a):
    return pltpu.with_memory_space_constraint(a, pltpu.HBM)


def pass_kernel(*refs):
    del refs


def after(a, *others):
    return pl.pallas_call(
        pass_kernel,
        out_shape=jax.ShapeDtypeStruct(a.shape, a.dtype),
        in_specs=[ANY] * (1 + len(others)),
        out_specs=ANY,
        input_output_aliases={0: 0},
        compiler_params=params(1),
        cost_estimate=cost(0, 0),
        name="after",
    )(a, *others)


def select_kernel(slot_cap, spans, tokens, grad_out, routes, order, *refs):
    sends, back = refs[: len(spans)], refs[len(spans)]
    xs, ys, route_in, order_in, sems = refs[len(spans) + 1 :]
    small = [
        pltpu.make_async_copy(routes, route_in, sems.at[0]),
        pltpu.make_async_copy(order, order_in, sems.at[1]),
    ]
    large = [
        pltpu.make_async_copy(tokens, xs, sems.at[2]),
        pltpu.make_async_copy(grad_out, ys, sems.at[3]),
    ]
    for copy in small + large:
        copy.start()
    count, width = tokens.shape
    rows = lax.broadcasted_iota(jnp.int32, (count, count), 0)
    lanes = lax.broadcasted_iota(jnp.int32, (count, count), 1)
    eye = rows == lanes
    me = lax.axis_index("expert")
    for copy in small:
        copy.wait()
    route_row = route_in[...]
    order_row = order_in[...]
    route_col = jnp.sum(jnp.where(eye, route_row, 0), axis=1, keepdims=True)
    order_col = jnp.sum(jnp.where(eye, order_row, 0), axis=1, keepdims=True)
    ahead = (route_col == route_row) & (order_col < order_row)
    rank = jnp.sum(ahead.astype(jnp.int32), axis=0, keepdims=True)
    place = jnp.bitwise_xor(route_row, me) * slot_cap + rank
    place = jnp.where(rank < slot_cap, place, -1)
    select = (rows == place).astype(F32).astype(BF16)
    place_col = jnp.sum(jnp.where(eye, place, 0), axis=1, keepdims=True)
    back[...] = (lanes == place_col).astype(F32).astype(BF16)
    for half, copy in enumerate(large):
        copy.wait()
        moved = jnp.dot(select, (xs, ys)[half][...], preferred_element_type=F32).astype(BF16)
        for send, (low, high) in zip(sends, spans):
            send[:, half * width : (half + 1) * width] = moved[low:high]


def select_rows(tokens, grad_out, routes, order, slot_cap, spans):
    count, width = tokens.shape
    return pl.pallas_call(
        functools.partial(select_kernel, slot_cap, spans),
        out_shape=[jax.ShapeDtypeStruct((high - low, 2 * width), BF16) for low, high in spans]
        + [jax.ShapeDtypeStruct((count, count), BF16)],
        in_specs=[HBM] * 4,
        out_specs=[VMEM] * (len(spans) + 1),
        scratch_shapes=[pltpu.VMEM((count, width), BF16)] * 2
        + [pltpu.VMEM((1, count), jnp.int32)] * 2
        + [pltpu.SemaphoreType.DMA((4,))],
        compiler_params=params(16),
        cost_estimate=cost(4 * count * count * width, 8 * count * width),
        name="select_rows",
    )(*map(in_hbm, (tokens, grad_out, routes.reshape(1, count), order)))


def load_kernel(gate_w, up_w, down_w, passed, pair_w, pair_t, down_t, passed_out, down_in, sems):
    del passed, passed_out
    width, units = gate_w.shape
    copies = [
        pltpu.make_async_copy(down_w, down_in, sems.at[0]),
        pltpu.make_async_copy(gate_w, pair_w.at[:, pl.ds(0, units)], sems.at[1]),
        pltpu.make_async_copy(up_w, pair_w.at[:, pl.ds(units, units)], sems.at[2]),
    ]
    for copy in copies:
        copy.start()
    tiles = width // units
    copies[0].wait()
    for t in range(tiles):
        part = slice(t * units, (t + 1) * units)
        down_t[part] = down_in[:, part].T
    for half in range(2):
        copies[1 + half].wait()
        side = slice(half * units, (half + 1) * units)
        for t in range(tiles):
            part = slice(t * units, (t + 1) * units)
            pair_t[side, part] = pair_w[part, side].T


def load_weights(gate_w, up_w, down_w, passed):
    width, units = gate_w.shape
    return pl.pallas_call(
        load_kernel,
        out_shape=[
            jax.ShapeDtypeStruct((width, 2 * units), BF16),
            jax.ShapeDtypeStruct((2 * units, width), BF16),
            jax.ShapeDtypeStruct((width, units), BF16),
            jax.ShapeDtypeStruct(passed.shape, passed.dtype),
        ],
        in_specs=[HBM] * 3 + [ANY],
        out_specs=[VMEM] * 3 + [ANY],
        scratch_shapes=[pltpu.VMEM((units, width), BF16), pltpu.SemaphoreType.DMA((3,))],
        input_output_aliases={3: 3},
        compiler_params=params(12),
        cost_estimate=cost(0, 0),
        name="load_weights",
    )(*map(in_hbm, (gate_w, up_w, down_w)), passed)


def chunk_kernel(n, first, *refs):
    blocks = refs[:n]
    pair_w, pair_t, down_t = refs[n : n + 3]
    xs, ys, hs, ps, away_out, keep_out = refs[-6:]
    width = pair_w.shape[0]
    units = down_t.shape[1]
    count = keep_out.shape[0]
    at = first
    for block in blocks:
        rows = block.shape[0]
        xs[at : at + rows] = block[:, :width]
        ys[at : at + rows] = block[:, width:]
        at += rows
    mine = slice(first, at)
    both = jnp.dot(xs[mine], pair_w[...], preferred_element_type=F32)
    gate, upper = both[:, :units], both[:, units:]
    sig = jax.nn.sigmoid(gate)
    active = gate * sig
    slope = sig * (1.0 + gate * (1.0 - sig))
    hs[mine] = (active * upper).astype(BF16)
    grad_hidden = jnp.dot(ys[mine], down_t[...], preferred_element_type=F32)
    ps[mine, :units] = (grad_hidden * upper * slope).astype(BF16)
    ps[mine, units:] = (grad_hidden * active).astype(BF16)
    back = jnp.dot(ps[mine], pair_t[...], preferred_element_type=F32)
    keep_out[...] = back[:count]
    away_out[...] = back[count:].astype(BF16)


def chunk_backward(blocks, weights, first, total, earlier, gates):
    n = len(blocks)
    width, units = weights[2].shape
    count = sum(block.shape[0] for block in blocks) // 2
    aliases = {n + 3 + i: i for i in range(len(earlier))}
    return pl.pallas_call(
        functools.partial(chunk_kernel, n, first),
        out_shape=[
            jax.ShapeDtypeStruct((total, width), BF16),
            jax.ShapeDtypeStruct((total, width), BF16),
            jax.ShapeDtypeStruct((total, units), BF16),
            jax.ShapeDtypeStruct((total, 2 * units), BF16),
            jax.ShapeDtypeStruct((count, width), BF16),
            jax.ShapeDtypeStruct((count, width), F32),
        ],
        in_specs=[VMEM] * (n + 3 + len(earlier)) + [ANY] * len(gates),
        out_specs=[VMEM] * 6,
        input_output_aliases=aliases,
        compiler_params=params(16),
        cost_estimate=cost(20 * count * width * units, 6 * width * units),
        name="chunk_backward",
    )(*blocks, *weights, *earlier, *gates)


def pair_kernel(xs, ps, before, gate_out, up_out, results, sems):
    del before
    units = gate_out.shape[1]
    part = xs.shape[1] // PAIR_TILES
    copies = []
    for t in range(PAIR_TILES):
        rows = slice(t * part, (t + 1) * part)
        both = lax.dot_general(xs[:, rows], ps[...], TN, preferred_element_type=F32)
        results[rows] = both.astype(BF16)
        for i, out in enumerate((gate_out, up_out)):
            source = results.at[pl.ds(t * part, part), pl.ds(i * units, units)]
            copies.append(pltpu.make_async_copy(source, out.at[pl.ds(t * part, part)], sems.at[t, i]))
            copies[-1].start()
    for copy in copies:
        copy.wait()


def down_kernel(ys, hs, before, down_out, mark, results, sems):
    del before
    mark[...] = jnp.zeros_like(mark)
    part = ys.shape[1] // TILES
    copies = []
    for t in range(TILES):
        columns = slice(t * part, (t + 1) * part)
        tile = lax.dot_general(hs[...], ys[:, columns], TN, preferred_element_type=F32)
        results[:, columns] = tile.astype(BF16)
        place = pl.ds(t * part, part)
        copies.append(pltpu.make_async_copy(results.at[:, place], down_out.at[:, place], sems.at[t]))
        copies[-1].start()
    for copy in copies:
        copy.wait()


def pair_grads(xs, ps, before):
    total, width = xs.shape
    units = ps.shape[1] // 2
    return pl.pallas_call(
        pair_kernel,
        out_shape=[jax.ShapeDtypeStruct((width, units), BF16)] * 2,
        in_specs=[VMEM, VMEM, ANY],
        out_specs=[HBM] * 2,
        scratch_shapes=[pltpu.VMEM((width, 2 * units), BF16), pltpu.SemaphoreType.DMA((PAIR_TILES, 2))],
        compiler_params=params(16),
        cost_estimate=cost(4 * total * width * units, 4 * width * units),
        name="pair_grads",
    )(xs, ps, before)


def down_grads(ys, hs, before):
    total, width = ys.shape
    units = hs.shape[1]
    return pl.pallas_call(
        down_kernel,
        out_shape=[jax.ShapeDtypeStruct((units, width), BF16), jax.ShapeDtypeStruct((8, 128), F32)],
        in_specs=[VMEM, VMEM, ANY],
        out_specs=[HBM, VMEM],
        scratch_shapes=[pltpu.VMEM((units, width), BF16), pltpu.SemaphoreType.DMA((TILES,))],
        compiler_params=params(12),
        cost_estimate=cost(2 * total * width * units, 2 * width * units),
        name="down_grads",
    )(ys, hs, before)


def place_kernel(back, *refs):
    units, (out, results, sems) = refs[:-3], refs[-3:]
    part = out.shape[1] // TILES
    copies = []
    for t in range(TILES):
        columns = pl.ds(t * part, part)
        rows = jnp.concatenate([unit[:, columns] for unit in units], axis=0)
        results[:, columns] = jnp.dot(back[...], rows, preferred_element_type=F32).astype(BF16)
        copies.append(pltpu.make_async_copy(results.at[:, columns], out.at[:, columns], sems.at[t]))
        copies[-1].start()
    for copy in copies:
        copy.wait()


def place_rows(back, units):
    count, width = back.shape[0], units[0].shape[1]
    return pl.pallas_call(
        place_kernel,
        out_shape=jax.ShapeDtypeStruct((count, width), BF16),
        in_specs=[VMEM] * (1 + len(units)),
        out_specs=HBM,
        scratch_shapes=[pltpu.VMEM((count, width), BF16), pltpu.SemaphoreType.DMA((TILES,))],
        compiler_params=params(16),
        cost_estimate=cost(2 * count * count * width, 4 * count * width),
        name="place_rows",
    )(back, *units)


def on_device(tokens, grad_out, routes, order, w_gate, w_up, w_down):
    experts = lax.axis_size("expert")
    shards = lax.axis_size("et")
    local_tokens, width = tokens.shape
    slot_cap = local_tokens // experts
    rows = local_tokens // GROUPS

    def over_expert(a, k):
        if k == 0:
            return a
        return lax.ppermute(a, "expert", [(i, i ^ k) for i in range(experts)])

    def over_et(a, m):
        return lax.ppermute(a, "et", [(i, i ^ m) for i in range(shards)])

    def span(unit):
        group, first, parts = unit
        low = group * rows + first * rows // PARTS
        return low, low + parts * rows // PARTS

    def exchange(a, unit):
        low, high = span(unit)
        pieces = []
        at = low
        while at < high:
            k = at // slot_cap
            end = min(high, (k + 1) * slot_cap)
            whole_unit = (at, end) == (low, high)
            pieces.append(over_expert(a if whole_unit else a[at - low : end - low], k))
            at = end
        return pieces[0] if len(pieces) == 1 else jnp.concatenate(pieces, axis=0)

    units = [unit for piece in PIECES for unit in piece]
    spans = [span(unit) for unit in units]
    *sends, back = select_rows(tokens, grad_out, routes, order, slot_cap, spans)
    sends = dict(zip(units, sends))

    arrived = {}
    for unit in units:
        arrived[unit] = exchange(sends[unit], unit)

    weights = None
    ways = shards // 2
    kept, returned = {}, {}
    before, gates, returns = [], [], []
    everything, first = [], 0
    for step, piece in enumerate(PIECES):
        last = step == len(PIECES) - 1
        near = []
        for unit in piece:
            mine = [arrived[unit]]
            for m in range(2, shards, 2):
                mine.append(over_et(arrived[unit], m))
            if weights is None:
                *weights, mine[-1] = load_weights(w_gate[0], w_up[0], w_down[0], mine[-1])
            if last:
                mine[-1] = after(mine[-1], *before)
            near += mine
        far = [over_et(a, 1) for a in near]
        *everything, away, keep = chunk_backward(
            near + far, weights, first, shards * local_tokens, everything, before + gates
        )
        first += 2 * keep.shape[0]
        before = [away]
        many = keep.shape[0] // len(piece)
        for i, unit in enumerate(piece):
            kept[unit] = keep[i * many : (i + 1) * many], away[i * many : (i + 1) * many]
        for group in RETURNS[step]:
            own, sent = [], [[] for _ in range(ways - 1)]
            for unit in group:
                keep, away = kept[unit]
                summed = keep + over_et(away, 1).astype(F32)
                many = keep.shape[0] // ways
                own.append(summed[:many])
                for w in range(1, ways):
                    sent[w - 1].append(summed[w * many : (w + 1) * many].astype(BF16))
            own = jnp.concatenate(own, axis=0)
            sent = [jnp.concatenate(part, axis=0) for part in sent]
            if not gates:
                gates.append(sent[-1])
            returns.append((group, own, sent))
    xs, ys, hs, ps = everything
    down_grad, mark = down_grads(ys, hs, returns[-1][2][-1])
    done = {}
    for k in (0, 3, 1, 2):
        _, own, sent = returns[k]
        if k == 2:
            sent = [after(piece, mark) for piece in sent]
        for w, piece in enumerate(sent, 1):
            own = own + over_et(piece, 2 * w).astype(F32)
        done[k] = own.astype(BF16)
    for k, gate in ((0, None), (3, mark), (1, 3), (2, None)):
        if gate is not None:
            done[k] = after(done[k], done[gate] if k == 1 else gate)
        (unit,) = returns[k][0]
        returned[unit] = exchange(done[k], unit)
    gate_grad, up_grad = pair_grads(xs, ps, done[3])
    grad_tokens = place_rows(back, [returned[unit] for unit in sorted(units)])
    return grad_tokens, gate_grad[None], up_grad[None], down_grad[None]


def solution(mesh):
    return jax.shard_map(
        on_device,
        mesh=mesh,
        in_specs=(
            P(("groups", "expert", "et"), None),
            P(("groups", "expert", "et"), None),
            P(("groups", "expert", "et"), None),
            P(("groups", "expert", "et"), None),
            P("expert", None, "et"),
            P("expert", None, "et"),
            P("expert", "et", None),
        ),
        out_specs=(
            P(("groups", "expert", "et"), None),
            P(("groups", "expert"), None, "et"),
            P(("groups", "expert"), None, "et"),
            P(("groups", "expert"), "et", None),
        ),
        check_vma=False,
    )
```
